32 devices in a mesh: tok: 8 (over y, x, core), wid: 4 (over z).
Axes of the slice: x: 2, y: 2, z: 4, core: 2. Of those that a mesh axis runs over, the one named last changes fastest.
Arguments:
- patches: bfloat16 [1536, 8, 6144], P('tok', None, 'wid'), may hold values from -6 to 6
- w_query: bfloat16 [6144, 4096], P('tok', 'wid'), may hold values from -0.102062073 to 0.102062073
- w_key: bfloat16 [6144, 4096], P('tok', 'wid'), may hold values from -0.102062073 to 0.102062073
- w_value: bfloat16 [6144, 4096], P('tok', 'wid'), may hold values from -0.078125 to 0.078125
- q_gain: float32 [4096], P('wid'), may hold values from 0.5 to 6
- k_gain: float32 [4096], P('wid'), may hold values from 0.5 to 6
- w_out: bfloat16 [4096, 6144], P('tok', 'wid'), may hold values from -0.09375 to 0.09375
Outputs:
- layer_out: bfloat16 [1536, 8, 6144], P('tok', None, 'wid')
The draws below stay inside these ranges and needn't reach their ends.
All inputs are finite; a program needn't handle non-finite values.
Results may differ from the reference program's by a relative error of at most 0.0034.
The reference program's roundings to bfloat16 on the way (of `normed`, `value`, `probs` and `mixed`) count: a program that leaves them out, or rounds other values in their place, can miss the bound.
Values may be sent and summed in bfloat16 or wider, within the bound.
A program may use at most 192 MiB of HBM per device.

```python
import jax
import jax.numpy as jnp
from jax import lax

D = 6144
HEADS = 32
HEAD_DIM = 128
PATCHES = 1536
IMAGES = 8
HD = 4096


def base_query(key):
    raw = jnp.clip(jax.random.normal(jax.random.fold_in(key, 11), (D, HD), jnp.float32), -6.0, 6.0)
    return raw * D ** (-0.5)


def draw_w_query(key, part):
    return base_query(key).astype(jnp.bfloat16)


def draw_w_key(key, part):
    noise = jnp.clip(jax.random.normal(jax.random.fold_in(key, 12), (D, HD), jnp.float32), -6.0, 6.0)
    result = noise * D ** (-0.5)
    return result.astype(jnp.bfloat16)


def gain_draw(key, salt):
    result = jax.random.uniform(jax.random.fold_in(key, salt), (HD,), jnp.float32, 0.6, 1.4)
    return result


def draw_q_gain(key, part):
    return gain_draw(key, 21)


def draw_k_gain(key, part):
    return gain_draw(key, 31)


def level_of(key, extent, cuts, low, largest):
    loudness = 1.0
    for position, parts in cuts:
        steps = jax.random.uniform(jax.random.fold_in(jax.random.fold_in(key, 6), position), (parts,), jnp.float32, low / len(cuts), largest / len(cuts))
        loudness = loudness * jnp.repeat(jnp.exp(steps), extent[position] // parts).reshape((-1,) + (1,) * (len(extent) - 1 - position))
    return loudness


def gaussian(rng, extent, deviation, reach, cuts=(), kind=jnp.bfloat16):
    drawn = deviation * jax.random.normal(rng, extent, jnp.float32)
    if cuts:
        drawn = drawn * level_of(rng, extent, cuts, -0.22, 0.18)
    return jnp.clip(drawn, -reach, reach).astype(kind)


def setup_inputs(seed: int = 0) -> dict:
    seeds = jax.random.split(jax.random.key(seed), 8)
    return {
        "patches": gaussian(seeds[0], (PATCHES, IMAGES, D), 1.0, 6.0, ((0, 8), (2, 4))),
        "w_query": draw_w_query(jax.random.fold_in(seeds[7], 71), 0),
        "w_key": draw_w_key(jax.random.fold_in(seeds[7], 71), 0),
        "w_value": gaussian(seeds[3], (D, HD), D ** -0.5, 0.078125, ((0, 8), (1, 4))),
        "q_gain": draw_q_gain(jax.random.fold_in(seeds[7], 71), 0),
        "k_gain": draw_k_gain(jax.random.fold_in(seeds[7], 71), 0),
        "w_out": gaussian(seeds[6], (HD, D), HD ** -0.5, 0.09375, ((0, 8), (1, 4))),
    }


def layer_norm_rows(values, eps):
    mean = lax.optimization_barrier(jnp.mean(values, axis=-1, keepdims=True))
    var = lax.optimization_barrier(jnp.mean(values * values, axis=-1, keepdims=True)) - mean * mean
    return (values - mean) * lax.rsqrt(var + eps)

def reference(patches, w_query, w_key, w_value, q_gain, k_gain, w_out):
    flat = patches.reshape(PATCHES * IMAGES, D).astype(jnp.float32)
    normed = layer_norm_rows(flat, 1e-06).astype(jnp.bfloat16)
    query = jnp.dot(normed, w_query, preferred_element_type=jnp.float32)
    key = jnp.dot(normed, w_key, preferred_element_type=jnp.float32)
    value = jnp.dot(normed, w_value, preferred_element_type=jnp.float32).astype(jnp.bfloat16)
    query = query.reshape(PATCHES, IMAGES, HEADS, HEAD_DIM)
    key = key.reshape(PATCHES, IMAGES, HEADS, HEAD_DIM)
    qnorm = (layer_norm_rows(query, 1e-06) * q_gain.reshape(HEADS, HEAD_DIM)).astype(jnp.bfloat16)
    knorm = (layer_norm_rows(key, 1e-06) * k_gain.reshape(HEADS, HEAD_DIM)).astype(jnp.bfloat16)
    value = value.reshape(PATCHES, IMAGES, HEADS, HEAD_DIM)
    items_q = jnp.transpose(qnorm.reshape(PATCHES, IMAGES * HEADS, HEAD_DIM), (1, 0, 2))
    items_k = jnp.transpose(knorm.reshape(PATCHES, IMAGES * HEADS, HEAD_DIM), (1, 0, 2))
    items_v = jnp.transpose(value.reshape(PATCHES, IMAGES * HEADS, HEAD_DIM), (1, 0, 2))
    scale = HEAD_DIM ** (-0.5)

    def attend(triple):
        qitem, kitem, vitem = triple
        scores = jnp.dot(qitem.astype(jnp.float32), kitem.astype(jnp.float32).T) * scale
        top = lax.optimization_barrier(jnp.max(scores, axis=-1, keepdims=True))
        expo = jnp.exp(scores - top)
        probs = (expo / lax.optimization_barrier(jnp.sum(expo, axis=-1, keepdims=True))).astype(jnp.bfloat16)
        return jnp.dot(probs, vitem, preferred_element_type=jnp.float32).astype(jnp.bfloat16)
    mixed = lax.map(attend, (items_q, items_k, items_v))
    mixed = jnp.transpose(mixed, (1, 0, 2)).reshape(PATCHES * IMAGES, HD)
    branch = jnp.dot(mixed, w_out, preferred_element_type=jnp.float32)
    return (flat + branch).astype(jnp.bfloat16).reshape(PATCHES, IMAGES, D)
```

```python
import jax
import jax.numpy as jnp
from jax import lax
from jax.experimental import pallas as pl
from jax.experimental.pallas import tpu as pltpu
from jax.sharding import PartitionSpec as P

HEAD_DIM = 128
EPS = 1e-06


def layer_norm_rows(values, eps):
    mean = jnp.mean(values, axis=-1, keepdims=True)
    var = jnp.mean(values * values, axis=-1, keepdims=True) - mean * mean
    return (values - mean) * lax.rsqrt(var + eps)


def xor_gather(block, axis, count, order):
    keys = [0]
    data = block[None]
    pieces = {0: (data, 0)}
    for bit in order:
        step = 1 << bit
        got = lax.ppermute(data, axis, [(i, i ^ step) for i in range(count)])
        for slot, key in enumerate(keys):
            pieces[key ^ step] = (got, slot)
        keys = keys + [key ^ step for key in keys]
        if len(keys) < count:
            data = jnp.concatenate([data, got], axis=0)
    return [pieces[j][0][pieces[j][1]] for j in range(count)]


def gather_rows(weight, axis, count):
    bits = count.bit_length() - 1
    half = weight.shape[0] // 2
    first = xor_gather(weight[:half], axis, count, list(range(1, bits)) + [0])
    second = xor_gather(weight[half:], axis, count, list(range(bits - 1, 0, -1)) + [0])
    return jnp.concatenate([x for pair in zip(first, second) for x in pair], axis=0)


def xor_columns(whole, me, count):
    parts, columns = whole.shape[0], whole.shape[-1]
    per = count // parts
    width = columns // per
    sizes = (1,) + whole.shape[1:-1] + (width,)
    blocks = []
    for j in range(count):
        b = me ^ j
        start = (b // per,) + (0,) * (whole.ndim - 2) + ((b % per) * width,)
        blocks.append(lax.dynamic_slice(whole, start, sizes)[0])
    return blocks


def attend_kernel(q_ref, k_ref, v_ref, o_ref):
    near = (((1,), (1,)), ((), ()))
    far = (((1,), (0,)), ((), ()))
    q = q_ref[...].reshape(-1, HEAD_DIM)
    k = k_ref[...].reshape(-1, HEAD_DIM)
    v = v_ref[...].reshape(-1, HEAD_DIM)
    scores = lax.dot_general(q, k, near, preferred_element_type=jnp.float32) * HEAD_DIM ** (-0.5)
    expo = jnp.exp(scores - jnp.max(scores, axis=-1, keepdims=True))
    probs = (expo * (1.0 / jnp.sum(expo, axis=-1, keepdims=True))).astype(jnp.bfloat16)
    mixed = lax.dot_general(probs, v, far, preferred_element_type=jnp.float32)
    o_ref[...] = mixed.astype(jnp.bfloat16).reshape(o_ref.shape)


def attend(full):
    toks, items, _, rows, _ = full.shape
    step = max(1, 384 // rows)
    tall = toks * rows
    return pl.pallas_call(
        attend_kernel,
        grid=(items, toks // step),
        in_specs=[
            pl.BlockSpec((step, None, None, rows, HEAD_DIM), lambda i, t: (t, i, 0, 0, 0)),
            pl.BlockSpec((toks, None, None, rows, HEAD_DIM), lambda i, t: (0, i, 1, 0, 0)),
            pl.BlockSpec((toks, None, None, rows, HEAD_DIM), lambda i, t: (0, i, 2, 0, 0)),
        ],
        out_specs=pl.BlockSpec((step, None, rows, HEAD_DIM), lambda i, t: (t, i, 0, 0)),
        out_shape=jax.ShapeDtypeStruct((toks, items, rows, HEAD_DIM), jnp.bfloat16),
        compiler_params=pltpu.CompilerParams(vmem_limit_bytes=32 * 1024 * 1024),
        cost_estimate=pl.CostEstimate(
            flops=4 * items * tall * tall * HEAD_DIM,
            bytes_accessed=8 * items * tall * HEAD_DIM,
            transcendentals=items * tall * tall,
        ),
        name="attend",
    )(full, full, full)


def solution(mesh):
    toks, wids = mesh.shape["tok"], mesh.shape["wid"]

    def local(patches, w_query, w_key, w_value, q_gain, k_gain, w_out):
        rows, images, local_width = patches.shape
        me = lax.axis_index("tok")
        head_width = w_query.shape[1]
        heads = head_width // HEAD_DIM
        model = local_width * wids
        group = max(2, toks // heads)
        groups = images // group
        items = group * heads // toks

        mine = [
            jnp.transpose(patches[:, g * group : (g + 1) * group], (1, 0, 2)) for g in range(groups)
        ]
        wholes = [lax.all_gather(m, "wid", axis=0, tiled=False) for m in mine]
        w_in = gather_rows(jnp.concatenate([w_query, w_key, w_value], axis=1), "tok", toks)
        w_last = gather_rows(w_out, "tok", toks)

        outs = []
        for g in range(groups):
            whole = wholes[g]
            as_float = whole.astype(jnp.float32)
            mean = jnp.sum(as_float, axis=(0, 3)) / model
            var = jnp.sum(as_float * as_float, axis=(0, 3)) / model - mean * mean
            inv = lax.rsqrt(var + EPS)
            normed = jnp.concatenate(
                [
                    ((b.astype(jnp.float32) - mean[..., None]) * inv[..., None]).astype(jnp.bfloat16)
                    for b in xor_columns(whole, me, toks)
                ],
                axis=-1,
            ).reshape(group * rows, model)
            qkv = jnp.dot(normed, w_in, preferred_element_type=jnp.float32)
            qkv = qkv.reshape(group, rows, 3, heads, HEAD_DIM)
            qn = (layer_norm_rows(qkv[:, :, 0], EPS) * q_gain.reshape(heads, HEAD_DIM)).astype(jnp.bfloat16)
            kn = (layer_norm_rows(qkv[:, :, 1], EPS) * k_gain.reshape(heads, HEAD_DIM)).astype(jnp.bfloat16)
            vb = qkv[:, :, 2].astype(jnp.bfloat16)
            packed = jnp.stack([qn, kn, vb], axis=0)
            packed = jnp.transpose(packed, (1, 3, 0, 2, 4)) if heads < toks else jnp.transpose(packed, (3, 1, 0, 2, 4))
            packed = packed.reshape(toks, items, 3, rows, HEAD_DIM)
            full = lax.all_to_all(packed, "tok", split_axis=0, concat_axis=0, tiled=False)
            back = lax.all_to_all(attend(full), "tok", split_axis=0, concat_axis=0, tiled=False)
            if heads < toks:
                back = jnp.transpose(back.reshape(group, heads, rows, HEAD_DIM), (0, 2, 1, 3))
            else:
                back = jnp.transpose(back.reshape(heads, group, rows, HEAD_DIM), (1, 2, 0, 3))
            mixed = back.reshape(group * rows, head_width)
            every = lax.all_gather(mixed, "wid", axis=0, tiled=False)
            every = jnp.concatenate(xor_columns(every, me, toks), axis=-1)
            branch = jnp.dot(every, w_last, preferred_element_type=jnp.float32)
            out = mine[g].astype(jnp.float32) + branch.reshape(group, rows, local_width)
            outs.append(jnp.transpose(out.astype(jnp.bfloat16), (1, 0, 2)))
        return jnp.concatenate(outs, axis=1)

    placed = (
        P("tok", None, "wid"),
        P("tok", "wid"),
        P("tok", "wid"),
        P("tok", "wid"),
        P("wid"),
        P("wid"),
        P("tok", "wid"),
    )
    return jax.shard_map(
        local, mesh=mesh, in_specs=placed, out_specs=P("tok", None, "wid"), check_vma=False
    )
```

```python
import jax
import jax.numpy as jnp
from jax import lax
from jax.experimental import pallas as pl
from jax.experimental.pallas import tpu as pltpu
from jax.sharding import PartitionSpec as P

HEAD_DIM = 128
EPS = 1e-06


def layer_norm_rows(values, eps):
    mean = jnp.mean(values, axis=-1, keepdims=True)
    var = jnp.mean(values * values, axis=-1, keepdims=True) - mean * mean
    return (values - mean) * lax.rsqrt(var + eps)


def xor_gather(block, axis, count, order):
    keys = [0]
    data = block[None]
    pieces = {0: (data, 0)}
    for bit in order:
        step = 1 << bit
        got = lax.ppermute(data, axis, [(i, i ^ step) for i in range(count)])
        for slot, key in enumerate(keys):
            pieces[key ^ step] = (got, slot)
        keys = keys + [key ^ step for key in keys]
        if len(keys) < count:
            data = jnp.concatenate([data, got], axis=0)
    return [pieces[j][0][pieces[j][1]] for j in range(count)]


def gather_rows(weight, axis, count):
    bits = count.bit_length() - 1
    half = weight.shape[0] // 2
    first = xor_gather(weight[:half], axis, count, list(range(1, bits)) + [0])
    second = xor_gather(weight[half:], axis, count, list(range(bits - 1, 0, -1)) + [0])
    return jnp.concatenate([x for pair in zip(first, second) for x in pair], axis=0)


def xor_columns(whole, me, count):
    parts, columns = whole.shape[0], whole.shape[-1]
    per = count // parts
    width = columns // per
    sizes = (1,) + whole.shape[1:-1] + (width,)
    blocks = []
    for j in range(count):
        b = me ^ j
        start = (b // per,) + (0,) * (whole.ndim - 2) + ((b % per) * width,)
        blocks.append(lax.dynamic_slice(whole, start, sizes)[0])
    return blocks


def attend_kernel(q_ref, k_ref, v_ref, o_ref):
    near = (((1,), (1,)), ((), ()))
    far = (((1,), (0,)), ((), ()))
    q = q_ref[...].reshape(-1, HEAD_DIM)
    k = k_ref[...].reshape(-1, HEAD_DIM)
    v = v_ref[...].reshape(-1, HEAD_DIM)
    scores = lax.dot_general(q, k, near, preferred_element_type=jnp.float32) * HEAD_DIM ** (-0.5)
    expo = jnp.exp(scores - jnp.max(scores, axis=-1, keepdims=True))
    probs = (expo * (1.0 / jnp.sum(expo, axis=-1, keepdims=True))).astype(jnp.bfloat16)
    mixed = lax.dot_general(probs, v, far, preferred_element_type=jnp.float32)
    o_ref[...] = mixed.astype(jnp.bfloat16).reshape(o_ref.shape)


def attend(full):
    toks, items, _, rows, _ = full.shape
    step = max(1, 384 // rows)
    tall = toks * rows
    return pl.pallas_call(
        attend_kernel,
        grid=(items, toks // step),
        in_specs=[
            pl.BlockSpec((step, None, None, rows, HEAD_DIM), lambda i, t: (t, i, 0, 0, 0)),
            pl.BlockSpec((toks, None, None, rows, HEAD_DIM), lambda i, t: (0, i, 1, 0, 0)),
            pl.BlockSpec((toks, None, None, rows, HEAD_DIM), lambda i, t: (0, i, 2, 0, 0)),
        ],
        out_specs=pl.BlockSpec((step, None, rows, HEAD_DIM), lambda i, t: (t, i, 0, 0)),
        out_shape=jax.ShapeDtypeStruct((toks, items, rows, HEAD_DIM), jnp.bfloat16),
        compiler_params=pltpu.CompilerParams(vmem_limit_bytes=32 * 1024 * 1024),
        cost_estimate=pl.CostEstimate(
            flops=4 * items * tall * tall * HEAD_DIM,
            bytes_accessed=8 * items * tall * HEAD_DIM,
            transcendentals=items * tall * tall,
        ),
        name="attend",
    )(full, full, full)


def solution(mesh):
    toks, wids = mesh.shape["tok"], mesh.shape["wid"]

    def local(patches, w_query, w_key, w_value, q_gain, k_gain, w_out):
        rows, images, local_width = patches.shape
        me = lax.axis_index("tok")
        head_width = w_query.shape[1]
        heads = head_width // HEAD_DIM
        model = local_width * wids
        group = max(2, toks // heads)
        groups = images // group
        items = group * heads // toks

        mine = [
            jnp.transpose(patches[:, g * group : (g + 1) * group], (1, 0, 2)) for g in range(groups)
        ]
        wholes = [lax.all_gather(m, "wid", axis=0, tiled=False) for m in mine]
        w_in = gather_rows(jnp.concatenate([w_query, w_key, w_value], axis=1), "tok", toks)
        w_in, w_out = lax.optimization_barrier((w_in, w_out))
        w_last = gather_rows(w_out, "tok", toks)

        projected = []
        for g in range(groups):
            whole = wholes[g]
            if g == groups - 1 and g > 0:
                whole, projected[g - 1] = lax.optimization_barrier((whole, projected[g - 1]))
            as_float = whole.astype(jnp.float32)
            mean = jnp.sum(as_float, axis=(0, 3)) / model
            var = jnp.sum(as_float * as_float, axis=(0, 3)) / model - mean * mean
            inv = lax.rsqrt(var + EPS)
            normed = jnp.concatenate(
                [
                    ((b.astype(jnp.float32) - mean[..., None]) * inv[..., None]).astype(jnp.bfloat16)
                    for b in xor_columns(whole, me, toks)
                ],
                axis=-1,
            ).reshape(group * rows, model)
            product = jnp.dot(normed, w_in, preferred_element_type=jnp.float32)
            projected.append(lax.optimization_barrier(product))

        outs = []
        for g in range(groups):
            qkv = projected[g].reshape(group, rows, 3, heads, HEAD_DIM)
            qn = (layer_norm_rows(qkv[:, :, 0], EPS) * q_gain.reshape(heads, HEAD_DIM)).astype(jnp.bfloat16)
            kn = (layer_norm_rows(qkv[:, :, 1], EPS) * k_gain.reshape(heads, HEAD_DIM)).astype(jnp.bfloat16)
            vb = qkv[:, :, 2].astype(jnp.bfloat16)
            packed = jnp.stack([qn, kn, vb], axis=0)
            packed = jnp.transpose(packed, (1, 3, 0, 2, 4)) if heads < toks else jnp.transpose(packed, (3, 1, 0, 2, 4))
            packed = packed.reshape(toks, items, 3, rows, HEAD_DIM)
            full = lax.all_to_all(packed, "tok", split_axis=0, concat_axis=0, tiled=False)
            back = lax.all_to_all(attend(full), "tok", split_axis=0, concat_axis=0, tiled=False)
            if heads < toks:
                back = jnp.transpose(back.reshape(group, heads, rows, HEAD_DIM), (0, 2, 1, 3))
            else:
                back = jnp.transpose(back.reshape(heads, group, rows, HEAD_DIM), (1, 2, 0, 3))
            mixed = back.reshape(group * rows, head_width)
            every = lax.all_gather(mixed, "wid", axis=0, tiled=False)
            every = jnp.concatenate(xor_columns(every, me, toks), axis=-1)
            branch = jnp.dot(every, w_last, preferred_element_type=jnp.float32)
            out = mine[g].astype(jnp.float32) + branch.reshape(group, rows, local_width)
            outs.append(jnp.transpose(out.astype(jnp.bfloat16), (1, 0, 2)))
        return jnp.concatenate(outs, axis=1)

    placed = (
        P("tok", None, "wid"),
        P("tok", "wid"),
        P("tok", "wid"),
        P("tok", "wid"),
        P("wid"),
        P("wid"),
        P("tok", "wid"),
    )
    return jax.shard_map(
        local, mesh=mesh, in_specs=placed, out_specs=P("tok", None, "wid"), check_vma=False
    )
```
